32 devices in a mesh: tm: 8 (over y, x, core), space: 4 (over z).
Axes of the slice: x: 2, y: 2, z: 4, core: 2. Of those that a mesh axis runs over, the one named last changes fastest.
Arguments:
- state: float32 [16, 1024, 256], P('tm', 'space'), may hold values from -6 to 6
- forcing: float32 [16, 1024, 256], P('tm', 'space'), may hold values from -6 to 6
- jscale: float32 [1024], P('space'), may hold values from 0.5 to 2
- volume_kernel: float32 [256, 256], replicated, may hold values from -0.375 to 0.375
- neighbour: int32 [1024, 6], P('space'), may hold values from 0 to 383, as said below
- send_left: int32 [256], P('space'), may hold values from 0 to 255, as said below
- send_right: int32 [256], P('space'), may hold values from 0 to 255, as said below
Outputs:
- residual: float32 [16, 1024, 256], P('tm', 'space')
- new_state: float32 [16, 1024, 256], P('tm', 'space')
The draws below stay inside these ranges and needn't reach their ends.
Inputs may be any that keep to these rules, and one draw needn't show every extreme that they name: `neighbour`: entries of face 2 are below 320, those of face 3 are below 256 or at least 320, those of the other faces are below 256. `send_left`: each partition's 64 entries are different element numbers. `send_right`: each partition's 64 entries are different element numbers.
All inputs are finite; a program needn't handle non-finite values.
Results may differ from the reference program's by a relative error of at most 0.0003.
Values sent between devices are 32-bit elements; how exact they have to be, the bound alone decides.
A program may use at most 128 MiB of HBM per device.

```python
import math
import jax
import jax.numpy as jnp
from jax import lax

E_DEV = 256
COMP = 4
NODES = 64
HALO = 64
INST = 16
ELEMS = 1024
N_SPACE = 4


def draw_neighbour(key, part):
    key_inner, key_lower, key_upper = jax.random.split(key, 3)
    inner = jax.random.randint(key_inner, (ELEMS, 6), 0, E_DEV)
    lower = jax.random.randint(key_lower, (ELEMS,), 0, E_DEV + HALO)
    upper = jax.random.randint(key_upper, (ELEMS,), 0, E_DEV + HALO)
    upper = jnp.where(upper >= E_DEV, upper + HALO, upper)
    columns = jnp.arange(6)[None, :]
    table = jnp.where(columns == 2, lower[:, None], jnp.where(columns == 3, upper[:, None], inner))
    first_row = (jnp.arange(ELEMS) % E_DEV == 0)[:, None]
    table = jnp.where(first_row & (columns == 0), 0, table)
    table = jnp.where(first_row & (columns == 3), E_DEV + 2 * HALO - 1, table)
    return table.astype(jnp.int32)


def boundary_list(key):
    partitions = ELEMS // E_DEV
    keys = jax.random.split(key, partitions)

    def one_list(one_key):
        key_middle, key_order = jax.random.split(one_key)
        middle = jax.random.permutation(key_middle, E_DEV - 2) + 1
        chosen = jnp.concatenate([jnp.array([0, E_DEV - 1], dtype=jnp.int32), middle[:HALO - 2].astype(jnp.int32)])
        return jax.random.permutation(key_order, chosen)
    return jax.vmap(one_list)(keys).reshape(-1).astype(jnp.int32)


def draw_send_left(key, part):
    return boundary_list(jax.random.fold_in(key, 11))


def draw_send_right(key, part):
    return boundary_list(jax.random.fold_in(key, 23))


def levels(own_key, dims, cuts, low, high):
    gain, own = 1.0, jax.random.fold_in(own_key, 6)
    for dim, shards_of in cuts:
        draws = jnp.exp(jax.random.uniform(jax.random.fold_in(own, dim), (shards_of,), jnp.float32, low / len(cuts), high / len(cuts)))
        gain = gain * jnp.repeat(draws, dims[dim] // shards_of).reshape([-1 if axis == dim else 1 for axis in range(len(dims))])
    return gain


def bell_draw(own_key, shape, width, most, cuts=(), kind=jnp.bfloat16):
    level = levels(own_key, shape, cuts, -0.22, 0.18) if cuts else 1.0
    values = jax.random.normal(own_key, shape, jnp.float32) * width * level
    return jnp.minimum(jnp.maximum(values, -most), most).astype(kind)


def setup_inputs(seed: int = 0) -> dict:
    arg_keys = jax.random.split(jax.random.key(seed), 8)
    state = bell_draw(arg_keys[0], (INST, ELEMS, COMP * NODES), 1.0, 6.0, ((0, 8), (1, 4)), jnp.float32)
    forcing = bell_draw(arg_keys[1], (INST, ELEMS, COMP * NODES), 1.0, 6.0, ((0, 8), (1, 4)), jnp.float32)
    jscale = jnp.clip(jnp.exp(math.log(2.0) - 1.3862944 * jax.random.uniform(arg_keys[2], (ELEMS,), jnp.float32) ** levels(arg_keys[2], (ELEMS,), ((0, 4),), -0.2, 0.2)), 0.5, 2.0)
    volume_kernel = bell_draw(arg_keys[3], (COMP * NODES, COMP * NODES), (COMP * NODES) ** -0.5, 0.375, (), jnp.float32)
    neighbour = draw_neighbour(jax.random.fold_in(arg_keys[7], 71), 0)
    send_left = draw_send_left(jax.random.fold_in(arg_keys[7], 71), 0)
    send_right = draw_send_right(jax.random.fold_in(arg_keys[7], 71), 0)
    return dict(state=state, forcing=forcing, jscale=jscale, volume_kernel=volume_kernel, neighbour=neighbour, send_left=send_left, send_right=send_right)


lift_factor = 2.0
step_factor = 0.2


def spectral(offset, instances):
    lag_value = offset.astype(jnp.float32)
    parity = 1.0 - 2.0 * jnp.mod(offset, 2).astype(jnp.float32)
    angle_value = jnp.pi * lag_value / instances
    safe_sine = jnp.where(offset == 0, 1.0, jnp.sin(angle_value))
    return jnp.where(offset == 0, 0.0, 0.5 * parity * jnp.cos(angle_value) / safe_sine)


def face_trace(blocks, face_number):
    cube_view = blocks.reshape(blocks.shape[:-1] + (4, 4, 4, 4))
    node_index = 3 if face_number % 2 else 0
    normal_axis = face_number // 2
    if normal_axis == 0:
        picked = cube_view[..., :, node_index, :, :]
    elif normal_axis == 1:
        picked = cube_view[..., :, :, node_index, :]
    else:
        picked = cube_view[..., :, :, :, node_index]
    return picked.reshape(blocks.shape[:-1] + (64,))


def place_face(surface, penalty, face_number):
    shaped = penalty.reshape(penalty.shape[:-1] + (4, 4, 4))
    node_index = 3 if face_number % 2 else 0
    normal_axis = face_number // 2
    if normal_axis == 0:
        return surface.at[..., :, node_index, :, :].add(shaped)
    if normal_axis == 1:
        return surface.at[..., :, :, node_index, :].add(shaped)
    return surface.at[..., :, :, :, node_index].add(shaped)


def numerical_flux_penalty(minus, exterior_trace, face_number):
    jump_value = (exterior_trace - minus).reshape(minus.shape[:-1] + (4, 16))
    normal_sign = 1.0 if face_number % 2 else -1.0
    normal_axis = face_number // 2
    penalty = -0.5 * jump_value
    pressure_term = penalty[..., 0, :] + 0.5 * normal_sign * jump_value[..., 1 + normal_axis, :]
    velocity_term = penalty[..., 1 + normal_axis, :] + 0.5 * normal_sign * jump_value[..., 0, :]
    penalty = penalty.at[..., 0, :].set(pressure_term)
    penalty = penalty.at[..., 1 + normal_axis, :].set(velocity_term)
    return penalty.reshape(minus.shape)


def spatial_term(blocks, element_scale, table_rows, halo_left, halo_right, volume_kernel):
    local_count = blocks.shape[0]
    element_count = blocks.shape[1]
    halo_count = halo_left.shape[1]
    volume = jnp.einsum("iek,kl->iel", blocks, volume_kernel, precision=lax.Precision.HIGHEST)
    trace_values = [face_trace(blocks, face_number) for face_number in range(6)]
    padding = jnp.zeros((local_count, halo_count, 64), jnp.float32)
    surface = jnp.zeros((local_count, element_count, 4, 4, 4, 4), jnp.float32)
    for face_number in range(6):
        left_part = halo_left if face_number == 2 else padding
        right_part = halo_right if face_number == 3 else padding
        across = jnp.concatenate([trace_values[face_number ^ 1], left_part, right_part], axis=1)
        exterior_trace = jnp.take(across, table_rows[:, face_number].astype(jnp.int32), axis=1)
        penalty = numerical_flux_penalty(trace_values[face_number], exterior_trace, face_number)
        surface = place_face(surface, penalty, face_number)
    surface = surface.reshape(local_count, element_count, -1)
    return element_scale[None, :, None] * (volume + lift_factor * surface)


def reference(state, forcing, jscale, volume_kernel, neighbour, send_left, send_right):
    cells = state.shape[-1]
    grouped = state.reshape(INST, N_SPACE, E_DEV, cells).transpose(1, 0, 2, 3)
    forced = forcing.reshape(INST, N_SPACE, E_DEV, cells).transpose(1, 0, 2, 3)
    lists_left = send_left.reshape(N_SPACE, HALO).astype(jnp.int32)
    lists_right = send_right.reshape(N_SPACE, HALO).astype(jnp.int32)

    def pick_rows(blocks, rows):
        return jnp.take(blocks, rows, axis=1)

    picked_right = jax.vmap(pick_rows)(grouped, lists_right)
    picked_left = jax.vmap(pick_rows)(grouped, lists_left)
    from_left = jnp.roll(picked_right, 1, axis=0)
    from_right = jnp.roll(picked_left, -1, axis=0)
    all_rows = jnp.arange(INST, dtype=jnp.int32)
    weights = spectral(all_rows[:, None] - all_rows[None, :], INST)

    def one_partition(inputs):
        blocks, source, element_scale, table_rows, left_blocks, right_blocks = inputs
        deriv = jnp.einsum("nm,mek->nek", weights, blocks, precision=lax.Precision.HIGHEST)
        spatial = spatial_term(blocks, element_scale, table_rows, face_trace(left_blocks, 3),
                               face_trace(right_blocks, 2), volume_kernel)
        resid = deriv + spatial - source
        updated_state = blocks - (step_factor / element_scale)[None, :, None] * resid
        return resid, updated_state

    resid, updated_state = lax.map(one_partition, (grouped, forced, jscale.reshape(N_SPACE, E_DEV),
                                             neighbour.reshape(N_SPACE, E_DEV, 6), from_left, from_right))
    resid = resid.transpose(1, 0, 2, 3).reshape(INST, ELEMS, cells)
    updated_state = updated_state.transpose(1, 0, 2, 3).reshape(INST, ELEMS, cells)
    return resid, updated_state
```

```python
import functools

import jax
import jax.numpy as jnp
import numpy as np
from jax import lax
from jax.experimental import pallas as pl
from jax.experimental.pallas import tpu as pltpu
from jax.sharding import PartitionSpec as P

lift_factor = 2.0
step_factor = 0.2
CELLS = 256
HALO = 64
MESH = pl.DeviceIdType.MESH
F32, BF16 = jnp.float32, jnp.bfloat16


def face_nodes(face):
    end, axis = (3 if face % 2 else 0), face // 2
    cube = np.arange(64).reshape(4, 4, 4)
    return np.take(cube, end, axis=axis).reshape(-1)


def flux_table(source_face, face):
    source, target = face_nodes(source_face), face_nodes(face)
    sign, axis = (1.0 if face % 2 else -1.0), face // 2
    mix = -np.eye(4)
    mix[1 + axis, 0] += sign
    mix[0, 1 + axis] += sign
    table = np.zeros((4, 64, 4, 64))
    for a in range(16):
        table[:, source[a], :, target[a]] = 0.5 * lift_factor * mix
    return table.reshape(256, 256)


def lag_table(instances):
    lag = np.arange(-(instances - 1), instances)
    angle = np.pi * lag / instances
    sine = np.where(lag == 0, 1.0, np.sin(angle))
    value = 0.5 * (1.0 - 2.0 * (lag % 2)) * np.cos(angle) / sine
    return np.where(lag == 0, 0.0, value).astype(np.float32)


def halves(value):
    high = value.astype(BF16)
    return high, (value - high.astype(F32)).astype(BF16)


def dot(a, b):
    return jnp.dot(a, b, preferred_element_type=F32)


def kernel(sizes, lags, state, volume_kernel, minus, plus, neighbour, jscale, send_left, send_right, out,
           pack, split, acc, give, halo, g0, g1, p0, p1, r0, r1,
           hs, hr, s10, q10, s11, q11, s20, q20, s21, q21):
    xs, ys, zs = sizes
    local, count, _ = state.shape
    quarter = count // 4
    instances = local * 2 * xs * ys
    t, z = lax.axis_index("tm"), lax.axis_index("space")
    core, chip = lax.rem(t, 2), lax.div(t, 2)
    x, y = lax.rem(chip, xs), lax.div(chip, xs)
    up, down = lax.rem(z + 1, zs), lax.rem(z + zs - 1, zs)

    def at(yy, xx, cc):
        return {"tm": (yy * xs + xx) * 2 + cc, "space": z}

    def turn(base, step, size):
        return lax.rem(base + step, size) if step else base

    def other(cc, step):
        return 1 - cc if step else cc

    row = [(dx, dc) for dx in range(xs) for dc in range(2)]
    column = [(dy, dc) for dy in range(ys) for dc in range(2)]
    peers = [at(y, turn(x, dx, xs), other(core, dc)) for dx, dc in row[1:]]
    peers += [at(turn(y, dy, ys), x, other(core, dc)) for dy, dc in column if dy]
    peers += [{"tm": t, "space": up}, {"tm": t, "space": down}]
    barrier = pltpu.get_barrier_semaphore()
    for peer in peers:
        pl.semaphore_signal(barrier, inc=1, device_id=peer, device_id_type=MESH)
    pl.semaphore_wait(barrier, len(peers))

    def rows(half, cc):
        return pl.ds(pl.multiple_of((2 * half + cc) * quarter, quarter), quarter)

    plans = (
        (row, column, x, y, xs, ys, g0, p0, r0, s10, q10, s20, q20),
        (column, row, y, x, ys, xs, g1, p1, r1, s11, q11, s21, q21),
    )

    def target(half, first, second, cc):
        return at(second, first, cc) if half == 0 else at(first, second, cc)

    def first_copy(half, step, sending):
        (along, _, me, fixed, size, _, g, _, _, s, q, _, _), (d, dc) = plans[half], step
        mate, mate_core = turn(me, d, size), other(core, dc)
        slot = (me, core) if sending else (mate, mate_core)
        return pltpu.make_async_remote_copy(
            src_ref=state.at[:, rows(half, mate_core)], dst_ref=g.at[slot],
            send_sem=s.at[mate, mate_core], recv_sem=q.at[slot],
            device_id=target(half, mate, fixed, mate_core), device_id_type=MESH)

    def second_copy(half, step, sending):
        (_, _, fixed, me, _, size, _, p, r, _, _, s, q), (d, dc) = plans[half], step
        mate, mate_core = turn(me, d, size), other(core, dc)
        slot = (core, me) if sending else (mate_core, mate)
        return pltpu.make_async_remote_copy(
            src_ref=p.at[mate, mate_core], dst_ref=r.at[slot],
            send_sem=s.at[mate, mate_core], recv_sem=q.at[slot],
            device_id=target(half, fixed, mate, mate_core), device_id_type=MESH)

    firsts = [(half, step) for half in (0, 1) for step in plans[half][0] if step[0]]
    firsts += [(half, (0, 1)) for half in (0, 1)]
    for half, step in firsts:
        first_copy(half, step, True).start()

    pack[0:6, :] = neighbour[...].astype(F32)
    pack[6:7, :] = jscale[...]
    pack[7:8, 0:HALO] = send_left[...].astype(F32)
    pack[7:8, HALO:2 * HALO] = send_right[...].astype(F32)
    pack[7:8, 2 * HALO:] = jnp.zeros((1, count - 2 * HALO), F32)
    columns = jnp.transpose(pack[...])
    numbers = columns.astype(jnp.int32)
    scale = columns[:, 6:7]

    for i in range(local):
        high, low = halves(state[i])
        split[:, 2 * i * CELLS:(2 * i + 1) * CELLS] = high
        split[:, (2 * i + 1) * CELLS:(2 * i + 2) * CELLS] = low

    listed = numbers[0:2 * HALO, 7:8]
    chosen = (listed == lax.broadcasted_iota(jnp.int32, (2 * HALO, count), 1)).astype(F32).astype(BF16)
    sent = dot(chosen, split[...])
    for i in range(local):
        value = sent[:, 2 * i * CELLS:(2 * i + 1) * CELLS] + sent[:, (2 * i + 1) * CELLS:(2 * i + 2) * CELLS]
        give[0, i] = value[0:HALO]
        give[1, i] = value[HALO:]

    def halo_copy(side):
        return pltpu.make_async_remote_copy(
            src_ref=give.at[side], dst_ref=halo.at[1 - side], send_sem=hs.at[side], recv_sem=hr.at[1 - side],
            device_id={"tm": t, "space": up if side else down}, device_id_type=MESH)

    for side in (0, 1):
        halo_copy(side).start()

    vh, vl = halves(volume_kernel[...] + minus[...])
    for i in range(local):
        high = split[:, 2 * i * CELLS:(2 * i + 1) * CELLS]
        low = split[:, (2 * i + 1) * CELLS:(2 * i + 2) * CELLS]
        acc[i] = dot(high, vh) + dot(low, vh) + dot(high, vl)
    lanes = lax.broadcasted_iota(jnp.int32, (count, count), 1)

    def add_face(face, picked):
        picked = picked.astype(BF16)
        for i in range(local):
            high = picked[:, 2 * i * CELLS:(2 * i + 1) * CELLS]
            low = picked[:, (2 * i + 1) * CELLS:(2 * i + 2) * CELLS]
            acc[i] += dot(high, plus[face]) + dot(low, plus[face])

    for face in range(6):
        hot = (numbers[:, face:face + 1] == lanes).astype(F32).astype(BF16)
        add_face(face, dot(hot, split[...]))

    for half in (0, 1):
        along, across, me, fixed, size, other_size, g, p, r, _, _, _, _ = plans[half]
        for step in along[1:]:
            first_copy(half, step, False).wait_recv()
        mine = rows(half, core)
        start = (2 * half + core) * quarter

        def number(first, second, cc):
            return (((second * xs + first) if half == 0 else (first * xs + second)) * 2 + cc) * local

        origins = [(turn(me, d, size), other(core, dc)) for d, dc in along]
        for d, dc in [step for step in across if step[0]] + [(0, 1), (0, 0)]:
            mate, mate_core = turn(fixed, d, other_size), other(core, dc)
            base = number(me, mate, mate_core)
            weights = [[[lags[base + n - number(first, fixed, cc) - m + instances - 1] for m in range(local)]
                        for first, cc in origins] for n in range(local)]

            def chunk(k, carry, d=d, dc=dc, mate=mate, mate_core=mate_core, weights=weights):
                here = pl.ds(pl.multiple_of(k * 16, 16), 16)
                totals = [None] * local
                for o, (first, cc) in enumerate(origins):
                    for m in range(local):
                        if o == 0:
                            value = state[m, pl.ds(pl.multiple_of(start + k * 16, 16), 16), :]
                        else:
                            value = g[first, cc, m, here, :]
                        for n in range(local):
                            term = weights[n][o][m] * value
                            totals[n] = term if totals[n] is None else totals[n] + term
                for n in range(local):
                    if d == 0 and dc == 0:
                        r[core, fixed, n, here, :] = totals[n]
                    else:
                        p[mate, mate_core, n, here, :] = totals[n]
                return carry

            lax.fori_loop(0, quarter // 16, chunk, 0)
            if (d, dc) != (0, 0):
                second_copy(half, (d, dc), True).start()

    for side, face in ((0, 2), (1, 3)):
        halo_copy(1 - side).wait_recv()
        first = count + side * HALO
        slots = lax.broadcasted_iota(jnp.int32, (count, HALO), 1) + first
        hot = (numbers[:, face:face + 1] == slots).astype(F32).astype(BF16)
        for i in range(local):
            high, low = halves(halo[side, i])
            for part in (high, low):
                acc[i] += dot(dot(hot, part).astype(BF16), plus[face])

    for half in (0, 1):
        across, other_size, r = plans[half][1], plans[half][5], plans[half][8]
        for step in [s for s in across if s != (0, 0)]:
            second_copy(half, step, False).wait_recv()
        for cc in range(2):
            low = (2 * half + cc) * quarter
            for i in range(local):
                total = r[cc, 0, i]
                for slot in range(1, other_size):
                    total = total + r[cc, slot, i]
                out[i, low:low + quarter, :] = total + scale[low:low + quarter] * acc[i, low:low + quarter, :]

    for half, step in firsts:
        first_copy(half, step, True).wait_send()
    for side in (0, 1):
        halo_copy(side).wait_send()
    for half in (0, 1):
        for step in [s for s in plans[half][1] if s != (0, 0)]:
            second_copy(half, step, True).wait_send()


def local_step(sizes, state, forcing, jscale, volume_kernel, neighbour, send_left, send_right):
    xs, ys, _ = sizes
    local, count, cells = state.shape
    quarter = count // 4
    instances = local * 2 * xs * ys
    lags = jnp.asarray(lag_table(instances))
    plus = jnp.asarray(np.stack([flux_table(f ^ 1, f) for f in range(6)]).astype(np.float32), BF16)
    minus = jnp.asarray(-sum(flux_table(f, f) for f in range(6)).astype(np.float32))
    block = (local, quarter, cells)
    sems = pltpu.SemaphoreType.DMA
    vmem = pl.BlockSpec(memory_space=pltpu.VMEM)
    term = pl.pallas_call(
        functools.partial(kernel, sizes),
        out_shape=jax.ShapeDtypeStruct(state.shape, F32),
        in_specs=[pl.BlockSpec(memory_space=pltpu.SMEM)] + [vmem] * 8,
        out_specs=vmem,
        scratch_shapes=[
            pltpu.VMEM((8, count), F32),
            pltpu.VMEM((count, 2 * local * cells), BF16),
            pltpu.VMEM(state.shape, F32),
            pltpu.VMEM((2, local, HALO, cells), F32),
            pltpu.VMEM((2, local, HALO, cells), F32),
            pltpu.VMEM((xs, 2) + block, F32),
            pltpu.VMEM((ys, 2) + block, F32),
            pltpu.VMEM((ys, 2) + block, F32),
            pltpu.VMEM((xs, 2) + block, F32),
            pltpu.VMEM((2, ys) + block, F32),
            pltpu.VMEM((2, xs) + block, F32),
            sems((2,)), sems((2,)),
            sems((xs, 2)), sems((xs, 2)),
            sems((ys, 2)), sems((ys, 2)),
            sems((ys, 2)), sems((2, ys)),
            sems((xs, 2)), sems((2, xs)),
        ],
        compiler_params=pltpu.CompilerParams(
            collective_id=0, has_side_effects=True, vmem_limit_bytes=48 * 2**20),
        cost_estimate=pl.CostEstimate(flops=4 * 10**9, bytes_accessed=4 * 2**20, transcendentals=0),
    )(lags, state, volume_kernel, minus, plus, neighbour.T, jscale.reshape(1, -1),
      send_left.reshape(1, -1), send_right.reshape(1, -1))
    residual = term - forcing
    return residual, state - (step_factor / jscale)[None, :, None] * residual


def solution(mesh):
    chips = mesh.shape["tm"] // 2
    xs = max(d for d in range(1, chips + 1) if chips % d == 0 and d * d <= chips)
    sizes = (xs, chips // xs, mesh.shape["space"])
    field = P("tm", "space", None)
    in_specs = (field, field, P("space"), P(), P("space", None), P("space"), P("space"))
    return jax.shard_map(functools.partial(local_step, sizes), mesh=mesh, in_specs=in_specs,
                         out_specs=(field, field), check_vma=False)
```

```python
import functools

import jax
import jax.numpy as jnp
import numpy as np
from jax import lax
from jax.experimental import pallas as pl
from jax.experimental.pallas import tpu as pltpu
from jax.sharding import PartitionSpec as P

lift_factor = 2.0
step_factor = 0.2
CELLS = 256
HALO = 64
GROUP = 128
CHUNKS = 2
MESH = pl.DeviceIdType.MESH
F32, BF16 = jnp.float32, jnp.bfloat16


def face_nodes(face):
    end, axis = (3 if face % 2 else 0), face // 2
    cube = np.arange(64).reshape(4, 4, 4)
    return np.take(cube, end, axis=axis).reshape(-1)


def flux_table(source_rows, face):
    target = face_nodes(face)
    sign, axis = (1.0 if face % 2 else -1.0), face // 2
    mix = -np.eye(4)
    mix[1 + axis, 0] += sign
    mix[0, 1 + axis] += sign
    table = np.zeros((256, 4, 64))
    for a in range(16):
        for c in range(4):
            table[source_rows[c, a], :, target[a]] = 0.5 * lift_factor * mix[c]
    return table.reshape(256, 256)


def block_rows(face):
    return np.arange(4)[:, None] * 64 + face_nodes(face)[None, :]


def tables():
    pick = np.zeros((256, 384))
    for face in range(6):
        pick[block_rows(face).reshape(-1), face * 64 + np.arange(64)] = 1.0
    place = np.concatenate([
        flux_table(np.arange(64).reshape(4, 16) + 64 * (1 - f % 2), f)[:GROUP] for f in range(6)])
    minus = -sum(flux_table(block_rows(f), f) for f in range(6))
    return pick, place, minus


def lag_table(instances):
    lag = np.arange(-(instances - 1), instances)
    angle = np.pi * lag / instances
    sine = np.where(lag == 0, 1.0, np.sin(angle))
    value = 0.5 * (1.0 - 2.0 * (lag % 2)) * np.cos(angle) / sine
    return np.where(lag == 0, 0.0, value).astype(np.float32)


def halves(value):
    high = value.astype(BF16)
    return high, (value - high.astype(F32)).astype(BF16)


def dot(a, b):
    return jnp.dot(a, b, preferred_element_type=F32)


def kernel(sizes, lags_hbm, state, volume_hbm, minus_hbm, pick_hbm, place_hbm, neighbour_hbm, jscale_hbm,
           left_hbm, right_hbm, out, pace,
           lags, own, volume_kernel, minus, pick, place, neighbour, jscale, send_left, send_right,
           pack, split, traces, picked, acc, give, halo, g0, g1, p0, p1, r0, r1,
           load, hs, hr, s10, q10, s11, q11, s20, q20, s21, q21):
    xs, ys, zs = sizes
    local, count, _ = own.shape
    sub = g0.shape[4]
    chunks = g0.shape[2]
    quarter = count // 4
    parts = 2 * local
    instances = local * 2 * xs * ys
    t, z = lax.axis_index("tm"), lax.axis_index("space")
    core, chip = lax.rem(t, 2), lax.div(t, 2)
    x, y = lax.rem(chip, xs), lax.div(chip, xs)
    up, down = lax.rem(z + 1, zs), lax.rem(z + zs - 1, zs)

    def at(yy, xx, cc):
        return {"tm": (yy * xs + xx) * 2 + cc, "space": z}

    def turn(base, step, size):
        return lax.rem(base + step, size) if step else base

    def other(cc, step):
        return 1 - cc if step else cc

    row = [(dx, dc) for dx in range(xs) for dc in range(2)]
    column = [(dy, dc) for dy in range(ys) for dc in range(2)]
    peers = [at(y, turn(x, dx, xs), other(core, dc)) for dx, dc in row[1:]]
    peers += [at(turn(y, dy, ys), x, other(core, dc)) for dy, dc in column if dy]
    peers += [{"tm": t, "space": up}, {"tm": t, "space": down}]
    barrier = pltpu.get_barrier_semaphore()
    for peer in peers:
        pl.semaphore_signal(barrier, inc=1, device_id=peer, device_id_type=MESH)

    loads = [pltpu.make_async_copy(a, b, load.at[k]) for k, (a, b) in enumerate((
        (neighbour_hbm, neighbour), (jscale_hbm, jscale), (left_hbm, send_left), (right_hbm, send_right),
        (state, own), (pick_hbm, pick), (lags_hbm, lags), (volume_hbm, volume_kernel), (minus_hbm, minus),
        (place_hbm, place)))]
    for one in loads:
        one.start()
    pl.semaphore_wait(barrier, len(peers))

    def rows(half, cc, k):
        return pl.ds(pl.multiple_of((2 * half + cc) * quarter + k * sub, sub), sub)

    plans = (
        (row, column, x, y, xs, ys, g0, p0, r0, s10, q10, s20, q20),
        (column, row, y, x, ys, xs, g1, p1, r1, s11, q11, s21, q21),
    )

    def target(half, first, second, cc):
        return at(second, first, cc) if half == 0 else at(first, second, cc)

    def first_copy(half, step, k, sending):
        (along, _, me, fixed, size, _, g, _, _, s, q, _, _), (d, dc) = plans[half], step
        mate, mate_core = turn(me, d, size), other(core, dc)
        slot = (me, core, k) if sending else (mate, mate_core, k)
        return pltpu.make_async_remote_copy(
            src_ref=state.at[:, rows(half, mate_core, k)], dst_ref=g.at[slot],
            send_sem=s.at[mate, mate_core, k], recv_sem=q.at[slot],
            device_id=target(half, mate, fixed, mate_core), device_id_type=MESH)

    def second_copy(half, step, k, sending):
        (_, _, fixed, me, _, size, _, p, r, _, _, s, q), (d, dc) = plans[half], step
        mate, mate_core = turn(me, d, size), other(core, dc)
        slot = (core, me, k) if sending else (mate_core, mate, k)
        return pltpu.make_async_remote_copy(
            src_ref=p.at[mate, mate_core, k], dst_ref=r.at[slot],
            send_sem=s.at[mate, mate_core, k], recv_sem=q.at[slot],
            device_id=target(half, fixed, mate, mate_core), device_id_type=MESH)

    firsts = []
    for k in range(chunks):
        firsts += [(half, step, k) for half in (0, 1) for step in plans[half][0] if step[0]]
        firsts += [(half, (0, 1), k) for half in (0, 1)]
    for one in firsts:
        first_copy(*one, True).start()

    for one in loads[:5]:
        one.wait()
    pack[0:6, :] = neighbour[...].astype(F32)
    pack[6:7, :] = jscale[...]
    pace[...] = step_factor / jscale[...]
    pack[7:8, 0:HALO] = send_left[...].astype(F32)
    pack[7:8, HALO:2 * HALO] = send_right[...].astype(F32)
    pack[7:8, 2 * HALO:] = jnp.zeros((1, count - 2 * HALO), F32)
    columns = jnp.transpose(pack[...])
    numbers = columns.astype(jnp.int32)
    scale = columns[:, 6:7]

    def hot(column, first, size, width):
        lanes = lax.broadcasted_iota(jnp.int32, (size, width), 1) + first
        return (column == lanes).astype(F32).astype(BF16)

    for i in range(local):
        high, low = halves(own[i])
        split[2 * i * count:(2 * i + 1) * count, :] = high
        split[(2 * i + 1) * count:(2 * i + 2) * count, :] = low
    loads[5].wait()
    for part in range(parts):
        found = dot(split[part * count:(part + 1) * count, :], pick[...]).astype(BF16)
        for axis in range(3):
            traces[axis, 0:count, part * GROUP:(part + 1) * GROUP] = found[:, axis * GROUP:(axis + 1) * GROUP]

    sent = dot(hot(numbers[0:2 * HALO, 7:8], 0, 2 * HALO, count), traces[1, 0:count, :])
    for i in range(local):
        value = sent[:, 2 * i * GROUP:(2 * i + 1) * GROUP] + sent[:, (2 * i + 1) * GROUP:(2 * i + 2) * GROUP]
        give[0, i] = value[0:HALO]
        give[1, i] = value[HALO:]

    def halo_copy(side):
        return pltpu.make_async_remote_copy(
            src_ref=give.at[side], dst_ref=halo.at[1 - side], send_sem=hs.at[side], recv_sem=hr.at[1 - side],
            device_id={"tm": t, "space": up if side else down}, device_id_type=MESH)

    for side in (0, 1):
        halo_copy(side).start()

    def gather(faces, width):
        for slot, face in enumerate(faces):
            found = dot(hot(numbers[:, face:face + 1], 0, count, width), traces[face // 2, 0:width, :]).astype(BF16)
            for part in range(parts):
                picked[part * count:(part + 1) * count, face * GROUP:(face + 1) * GROUP] = (
                    found[:, part * GROUP:(part + 1) * GROUP])

    def put(first, last, fresh=False):
        used = slice(first * GROUP, last * GROUP)
        for i in range(local):
            total = None if fresh else acc[i]
            for part in (2 * i, 2 * i + 1):
                term = dot(picked[part * count:(part + 1) * count, used], place[used, :])
                total = term if total is None else total + term
            acc[i] = total

    def volume():
        loads[7].wait()
        loads[8].wait()
        vh, vl = halves(volume_kernel[...] + minus[...].astype(F32))
        for i in range(local):
            high = split[2 * i * count:(2 * i + 1) * count, :]
            low = split[(2 * i + 1) * count:(2 * i + 2) * count, :]
            acc[i] = dot(high, vh) + dot(low, vh) + dot(high, vl)

    def partial(half, k):
        along, across, me, fixed, size, other_size, g, p, r, _, _, _, _ = plans[half]
        for step in along[1:]:
            first_copy(half, step, k, False).wait_recv()
        start = (2 * half + core) * quarter + k * sub

        def number(first, second, cc):
            return (((second * xs + first) if half == 0 else (first * xs + second)) * 2 + cc) * local

        origins = [(turn(me, d, size), other(core, dc)) for d, dc in along]
        for d, dc in [step for step in across if step[0]] + [(0, 1), (0, 0)]:
            mate, mate_core = turn(fixed, d, other_size), other(core, dc)
            base = number(me, mate, mate_core)
            weights = [[[lags[base + n - number(first, fixed, cc) - m + instances - 1] for m in range(local)]
                        for first, cc in origins] for n in range(local)]

            def step16(j, carry, d=d, dc=dc, mate=mate, mate_core=mate_core, weights=weights):
                here = pl.ds(pl.multiple_of(j * 16, 16), 16)
                totals = [None] * local
                for o, (first, cc) in enumerate(origins):
                    for m in range(local):
                        if o == 0:
                            value = own[m, pl.ds(pl.multiple_of(start + j * 16, 16), 16), :]
                        else:
                            value = g[first, cc, k, m, here, :]
                        for n in range(local):
                            term = weights[n][o][m] * value
                            totals[n] = term if totals[n] is None else totals[n] + term
                for n in range(local):
                    if d == 0 and dc == 0:
                        r[core, fixed, k, n, here, :] = totals[n]
                    else:
                        p[mate, mate_core, k, n, here, :] = totals[n]
                return carry

            lax.fori_loop(0, sub // 16, step16, 0)
            if (d, dc) != (0, 0):
                second_copy(half, (d, dc), k, True).start()

    volume()
    gather((0, 1), count)
    loads[6].wait()
    for k in range(chunks):
        for half in (0, 1):
            partial(half, k)
        if k == 0:
            gather((4, 5), count)
    loads[9].wait()
    put(0, 2)
    put(4, 6)

    for side in (0, 1):
        halo_copy(1 - side).wait_recv()
        first = count + side * HALO
        for i in range(local):
            high, low = halves(halo[side, i])
            traces[1, first:first + HALO, 2 * i * GROUP:(2 * i + 1) * GROUP] = high
            traces[1, first:first + HALO, (2 * i + 1) * GROUP:(2 * i + 2) * GROUP] = low
    gather((2, 3), count + 2 * HALO)
    put(2, 4)

    for k in range(chunks):
        for half in (0, 1):
            across, other_size, r = plans[half][1], plans[half][5], plans[half][8]
            for step in [s for s in across if s != (0, 0)]:
                second_copy(half, step, k, False).wait_recv()
            for cc in range(2):
                low = (2 * half + cc) * quarter + k * sub
                for i in range(local):
                    total = r[cc, 0, k, i]
                    for slot in range(1, other_size):
                        total = total + r[cc, slot, k, i]
                    out[i, low:low + sub, :] = total + scale[low:low + sub] * acc[i, low:low + sub, :]

    for one in firsts:
        first_copy(*one, True).wait_send()
    for side in (0, 1):
        halo_copy(side).wait_send()
    for k in range(chunks):
        for half in (0, 1):
            for step in [s for s in plans[half][1] if s != (0, 0)]:
                second_copy(half, step, k, True).wait_send()


def local_step(sizes, state, forcing, jscale, volume_kernel, neighbour, send_left, send_right):
    xs, ys, _ = sizes
    local, count, cells = state.shape
    quarter = count // 4
    sub = quarter // CHUNKS
    instances = local * 2 * xs * ys
    lags = jnp.asarray(lag_table(instances))
    pick, place, minus = [jnp.asarray(table.astype(np.float32), BF16) for table in tables()]
    block = (CHUNKS, local, sub, cells)
    sems = pltpu.SemaphoreType.DMA
    term, pace = pl.pallas_call(
        functools.partial(kernel, sizes),
        out_shape=(jax.ShapeDtypeStruct(state.shape, F32), jax.ShapeDtypeStruct((1, count), F32)),
        in_specs=[pl.BlockSpec(memory_space=pltpu.HBM)] * 10,
        out_specs=[pl.BlockSpec(memory_space=pltpu.VMEM)] * 2,
        scratch_shapes=[
            pltpu.SMEM(lags.shape, F32),
            pltpu.VMEM(state.shape, F32),
            pltpu.VMEM((cells, cells), F32),
            pltpu.VMEM(minus.shape, BF16),
            pltpu.VMEM(pick.shape, BF16),
            pltpu.VMEM(place.shape, BF16),
            pltpu.VMEM((6, count), jnp.int32),
            pltpu.VMEM((1, count), F32),
            pltpu.VMEM((1, HALO), jnp.int32),
            pltpu.VMEM((1, HALO), jnp.int32),
            pltpu.VMEM((8, count), F32),
            pltpu.VMEM((2 * local * count, cells), BF16),
            pltpu.VMEM((3, count + 2 * HALO, 2 * local * GROUP), BF16),
            pltpu.VMEM((2 * local * count, 6 * GROUP), BF16),
            pltpu.VMEM(state.shape, F32),
            pltpu.VMEM((2, local, HALO, GROUP), F32),
            pltpu.VMEM((2, local, HALO, GROUP), F32),
            pltpu.VMEM((xs, 2) + block, F32),
            pltpu.VMEM((ys, 2) + block, F32),
            pltpu.VMEM((ys, 2) + block, F32),
            pltpu.VMEM((xs, 2) + block, F32),
            pltpu.VMEM((2, ys) + block, F32),
            pltpu.VMEM((2, xs) + block, F32),
            sems((10,)), sems((2,)), sems((2,)),
            sems((xs, 2, CHUNKS)), sems((xs, 2, CHUNKS)),
            sems((ys, 2, CHUNKS)), sems((ys, 2, CHUNKS)),
            sems((ys, 2, CHUNKS)), sems((2, ys, CHUNKS)),
            sems((xs, 2, CHUNKS)), sems((2, xs, CHUNKS)),
        ],
        compiler_params=pltpu.CompilerParams(
            collective_id=0, has_side_effects=True, vmem_limit_bytes=60 * 2**20),
        cost_estimate=pl.CostEstimate(flops=3 * 10**9, bytes_accessed=4 * 2**20, transcendentals=0),
    )(lags, state, volume_kernel, minus, pick, place, neighbour.T, jscale.reshape(1, -1),
      send_left.reshape(1, -1), send_right.reshape(1, -1))
    residual = term - forcing
    return residual, state - pace.reshape(1, -1, 1) * residual


def solution(mesh):
    chips = mesh.shape["tm"] // 2
    xs = max(d for d in range(1, chips + 1) if chips % d == 0 and d * d <= chips)
    sizes = (xs, chips // xs, mesh.shape["space"])
    field = P("tm", "space", None)
    in_specs = (field, field, P("space"), P(), P("space", None), P("space"), P("space"))
    return jax.shard_map(functools.partial(local_step, sizes), mesh=mesh, in_specs=in_specs,
                         out_specs=(field, field), check_vma=False)
```

```python
import functools

import jax
import jax.numpy as jnp
import numpy as np
from jax import lax
from jax.experimental import pallas as pl
from jax.experimental.pallas import tpu as pltpu
from jax.sharding import PartitionSpec as P

lift_factor = 2.0
step_factor = 0.2
CELLS = 256
HALO = 64
GROUP = 128
CHUNKS = 2
MESH = pl.DeviceIdType.MESH
F32, BF16 = jnp.float32, jnp.bfloat16


def face_nodes(face):
    end, axis = (3 if face % 2 else 0), face // 2
    cube = np.arange(64).reshape(4, 4, 4)
    return np.take(cube, end, axis=axis).reshape(-1)


def flux_table(source_rows, face):
    target = face_nodes(face)
    sign, axis = (1.0 if face % 2 else -1.0), face // 2
    mix = -np.eye(4)
    mix[1 + axis, 0] += sign
    mix[0, 1 + axis] += sign
    table = np.zeros((256, 4, 64))
    for a in range(16):
        for c in range(4):
            table[source_rows[c, a], :, target[a]] = 0.5 * lift_factor * mix[c]
    return table.reshape(256, 256)


def block_rows(face):
    return np.arange(4)[:, None] * 64 + face_nodes(face)[None, :]


def tables():
    pick = np.zeros((256, 384))
    for face in range(6):
        pick[block_rows(face).reshape(-1), face * 64 + np.arange(64)] = 1.0
    place = np.concatenate([
        flux_table(np.arange(64).reshape(4, 16) + 64 * (1 - f % 2), f)[:GROUP] for f in range(6)])
    minus = -sum(flux_table(block_rows(f), f) for f in range(6))
    return pick, place, minus


def lag_table(instances):
    lag = np.arange(-(instances - 1), instances)
    angle = np.pi * lag / instances
    sine = np.where(lag == 0, 1.0, np.sin(angle))
    value = 0.5 * (1.0 - 2.0 * (lag % 2)) * np.cos(angle) / sine
    return np.where(lag == 0, 0.0, value).astype(np.float32)


def halves(value):
    high = value.astype(BF16)
    return high, (value - high.astype(F32)).astype(BF16)


def dot(a, b):
    return jnp.dot(a, b, preferred_element_type=F32)


def kernel(sizes, lags_hbm, state, volume_hbm, minus_hbm, pick_hbm, place_hbm, neighbour_hbm, jscale_hbm,
           left_hbm, right_hbm, out, pace,
           lags, own, volume_kernel, minus, pick, place, neighbour, jscale, send_left, send_right,
           pack, split, traces, picked, acc, give, halo, g0, g1, p0, p1, r0, r1,
           load, hs, hr, s10, q10, s11, q11, s20, q20, s21, q21):
    xs, ys, zs = sizes
    local, count, _ = own.shape
    sub = g0.shape[4]
    chunks = g0.shape[2]
    quarter = count // 4
    parts = 2 * local
    instances = local * 2 * xs * ys
    t, z = lax.axis_index("tm"), lax.axis_index("space")
    core, chip = lax.rem(t, 2), lax.div(t, 2)
    x, y = lax.rem(chip, xs), lax.div(chip, xs)
    up, down = lax.rem(z + 1, zs), lax.rem(z + zs - 1, zs)

    def at(yy, xx, cc):
        return {"tm": (yy * xs + xx) * 2 + cc, "space": z}

    def turn(base, step, size):
        return lax.rem(base + step, size) if step else base

    def other(cc, step):
        return 1 - cc if step else cc

    row = [(dx, dc) for dx in range(xs) for dc in range(2)]
    column = [(dy, dc) for dy in range(ys) for dc in range(2)]
    peers = [at(y, turn(x, dx, xs), other(core, dc)) for dx, dc in row[1:]]
    peers += [at(turn(y, dy, ys), x, other(core, dc)) for dy, dc in column if dy]
    peers += [{"tm": t, "space": up}, {"tm": t, "space": down}]
    barrier = pltpu.get_barrier_semaphore()
    for peer in peers:
        pl.semaphore_signal(barrier, inc=1, device_id=peer, device_id_type=MESH)

    loads = [pltpu.make_async_copy(a, b, load.at[k]) for k, (a, b) in enumerate((
        (neighbour_hbm, neighbour), (jscale_hbm, jscale), (left_hbm, send_left), (right_hbm, send_right),
        (state, own), (pick_hbm, pick), (lags_hbm, lags), (volume_hbm, volume_kernel), (minus_hbm, minus),
        (place_hbm, place)))]
    loads[4].start()
    for one in loads[:4] + loads[5:]:
        one.start()
    loads[4].wait()
    pl.semaphore_wait(barrier, len(peers))

    def rows(half, cc, k):
        return pl.ds(pl.multiple_of((2 * half + cc) * quarter + k * sub, sub), sub)

    plans = (
        (row, column, x, y, xs, ys, g0, p0, r0, s10, q10, s20, q20),
        (column, row, y, x, ys, xs, g1, p1, r1, s11, q11, s21, q21),
    )

    def target(half, first, second, cc):
        return at(second, first, cc) if half == 0 else at(first, second, cc)

    def first_copy(half, step, k, sending):
        (along, _, me, fixed, size, _, g, _, _, s, q, _, _), (d, dc) = plans[half], step
        mate, mate_core = turn(me, d, size), other(core, dc)
        slot = (me, core, k) if sending else (mate, mate_core, k)
        return pltpu.make_async_remote_copy(
            src_ref=own.at[:, rows(half, mate_core, k)], dst_ref=g.at[slot],
            send_sem=s.at[mate, mate_core, k], recv_sem=q.at[slot],
            device_id=target(half, mate, fixed, mate_core), device_id_type=MESH)

    def second_copy(half, step, k, sending):
        (_, _, fixed, me, _, size, _, p, r, _, _, s, q), (d, dc) = plans[half], step
        mate, mate_core = turn(me, d, size), other(core, dc)
        slot = (core, me, k) if sending else (mate_core, mate, k)
        return pltpu.make_async_remote_copy(
            src_ref=p.at[mate, mate_core, k], dst_ref=r.at[slot],
            send_sem=s.at[mate, mate_core, k], recv_sem=q.at[slot],
            device_id=target(half, fixed, mate, mate_core), device_id_type=MESH)

    firsts = []
    for k in range(chunks):
        firsts += [(half, step, k) for half in (0, 1) for step in plans[half][0] if step[0]]
        firsts += [(half, (0, 1), k) for half in (0, 1)]
    for one in firsts:
        first_copy(*one, True).start()

    for one in loads[:4]:
        one.wait()
    pack[0:6, :] = neighbour[...].astype(F32)
    pack[6:7, :] = jscale[...]
    pace[...] = step_factor / jscale[...]
    pack[7:8, 0:HALO] = send_left[...].astype(F32)
    pack[7:8, HALO:2 * HALO] = send_right[...].astype(F32)
    pack[7:8, 2 * HALO:] = jnp.zeros((1, count - 2 * HALO), F32)
    columns = jnp.transpose(pack[...])
    numbers = columns.astype(jnp.int32)
    scale = columns[:, 6:7]

    def hot(column, first, size, width):
        lanes = lax.broadcasted_iota(jnp.int32, (size, width), 1) + first
        return (column == lanes).astype(F32).astype(BF16)

    for i in range(local):
        high, low = halves(own[i])
        split[2 * i * count:(2 * i + 1) * count, :] = high
        split[(2 * i + 1) * count:(2 * i + 2) * count, :] = low
    loads[5].wait()
    for part in range(parts):
        found = dot(split[part * count:(part + 1) * count, :], pick[...]).astype(BF16)
        for axis in range(3):
            traces[axis, 0:count, part * GROUP:(part + 1) * GROUP] = found[:, axis * GROUP:(axis + 1) * GROUP]

    sent = dot(hot(numbers[0:2 * HALO, 7:8], 0, 2 * HALO, count), traces[1, 0:count, :])
    for i in range(local):
        value = sent[:, 2 * i * GROUP:(2 * i + 1) * GROUP] + sent[:, (2 * i + 1) * GROUP:(2 * i + 2) * GROUP]
        give[0, i] = value[0:HALO]
        give[1, i] = value[HALO:]

    def halo_copy(side):
        return pltpu.make_async_remote_copy(
            src_ref=give.at[side], dst_ref=halo.at[1 - side], send_sem=hs.at[side], recv_sem=hr.at[1 - side],
            device_id={"tm": t, "space": up if side else down}, device_id_type=MESH)

    for side in (0, 1):
        halo_copy(side).start()

    def gather(faces, width):
        for slot, face in enumerate(faces):
            found = dot(hot(numbers[:, face:face + 1], 0, count, width), traces[face // 2, 0:width, :]).astype(BF16)
            for part in range(parts):
                picked[part * count:(part + 1) * count, face * GROUP:(face + 1) * GROUP] = (
                    found[:, part * GROUP:(part + 1) * GROUP])

    def put(first, last, fresh=False):
        used = slice(first * GROUP, last * GROUP)
        for i in range(local):
            total = None if fresh else acc[i]
            for part in (2 * i, 2 * i + 1):
                term = dot(picked[part * count:(part + 1) * count, used], place[used, :])
                total = term if total is None else total + term
            acc[i] = total

    def volume():
        loads[7].wait()
        loads[8].wait()
        vh, vl = halves(volume_kernel[...] + minus[...].astype(F32))
        for i in range(local):
            high = split[2 * i * count:(2 * i + 1) * count, :]
            low = split[(2 * i + 1) * count:(2 * i + 2) * count, :]
            acc[i] = dot(high, vh) + dot(low, vh) + dot(high, vl)

    def partial(half, k):
        along, across, me, fixed, size, other_size, g, p, r, _, _, _, _ = plans[half]
        for step in along[1:]:
            first_copy(half, step, k, False).wait_recv()
        start = (2 * half + core) * quarter + k * sub

        def number(first, second, cc):
            return (((second * xs + first) if half == 0 else (first * xs + second)) * 2 + cc) * local

        origins = [(turn(me, d, size), other(core, dc)) for d, dc in along]
        for d, dc in [step for step in across if step[0]] + [(0, 1), (0, 0)]:
            mate, mate_core = turn(fixed, d, other_size), other(core, dc)
            base = number(me, mate, mate_core)
            weights = [[[lags[base + n - number(first, fixed, cc) - m + instances - 1] for m in range(local)]
                        for first, cc in origins] for n in range(local)]

            def step16(j, carry, d=d, dc=dc, mate=mate, mate_core=mate_core, weights=weights):
                here = pl.ds(pl.multiple_of(j * 16, 16), 16)
                totals = [None] * local
                for o, (first, cc) in enumerate(origins):
                    for m in range(local):
                        if o == 0:
                            value = own[m, pl.ds(pl.multiple_of(start + j * 16, 16), 16), :]
                        else:
                            value = g[first, cc, k, m, here, :]
                        for n in range(local):
                            term = weights[n][o][m] * value
                            totals[n] = term if totals[n] is None else totals[n] + term
                for n in range(local):
                    if d == 0 and dc == 0:
                        r[core, fixed, k, n, here, :] = totals[n]
                    else:
                        p[mate, mate_core, k, n, here, :] = totals[n]
                return carry

            lax.fori_loop(0, sub // 16, step16, 0)
            if (d, dc) != (0, 0):
                second_copy(half, (d, dc), k, True).start()

    volume()
    gather((0, 1), count)
    loads[6].wait()
    for k in range(chunks):
        for half in (0, 1):
            partial(half, k)
        if k == 0:
            gather((4, 5), count)
    loads[9].wait()
    put(0, 2)
    put(4, 6)

    for side in (0, 1):
        halo_copy(1 - side).wait_recv()
        first = count + side * HALO
        for i in range(local):
            high, low = halves(halo[side, i])
            traces[1, first:first + HALO, 2 * i * GROUP:(2 * i + 1) * GROUP] = high
            traces[1, first:first + HALO, (2 * i + 1) * GROUP:(2 * i + 2) * GROUP] = low
    gather((2, 3), count + 2 * HALO)
    put(2, 4)

    for k in range(chunks):
        for half in (0, 1):
            across, other_size, r = plans[half][1], plans[half][5], plans[half][8]
            for step in [s for s in across if s != (0, 0)]:
                second_copy(half, step, k, False).wait_recv()
            for cc in range(2):
                low = (2 * half + cc) * quarter + k * sub
                for i in range(local):
                    total = r[cc, 0, k, i]
                    for slot in range(1, other_size):
                        total = total + r[cc, slot, k, i]
                    out[i, low:low + sub, :] = total + scale[low:low + sub] * acc[i, low:low + sub, :]

    for one in firsts:
        first_copy(*one, True).wait_send()
    for side in (0, 1):
        halo_copy(side).wait_send()
    for k in range(chunks):
        for half in (0, 1):
            for step in [s for s in plans[half][1] if s != (0, 0)]:
                second_copy(half, step, k, True).wait_send()


def local_step(sizes, state, forcing, jscale, volume_kernel, neighbour, send_left, send_right):
    xs, ys, _ = sizes
    local, count, cells = state.shape
    quarter = count // 4
    sub = quarter // CHUNKS
    instances = local * 2 * xs * ys
    lags = jnp.asarray(lag_table(instances))
    pick, place, minus = [jnp.asarray(table.astype(np.float32), BF16) for table in tables()]
    block = (CHUNKS, local, sub, cells)
    sems = pltpu.SemaphoreType.DMA
    term, pace = pl.pallas_call(
        functools.partial(kernel, sizes),
        out_shape=(pltpu.VMEM(state.shape, F32), pltpu.VMEM((1, count), F32)),
        in_specs=[pl.BlockSpec(memory_space=pltpu.HBM)] * 10,
        out_specs=[pl.BlockSpec(memory_space=pltpu.VMEM)] * 2,
        scratch_shapes=[
            pltpu.SMEM(lags.shape, F32),
            pltpu.VMEM(state.shape, F32),
            pltpu.VMEM((cells, cells), F32),
            pltpu.VMEM(minus.shape, BF16),
            pltpu.VMEM(pick.shape, BF16),
            pltpu.VMEM(place.shape, BF16),
            pltpu.VMEM((6, count), jnp.int32),
            pltpu.VMEM((1, count), F32),
            pltpu.VMEM((1, HALO), jnp.int32),
            pltpu.VMEM((1, HALO), jnp.int32),
            pltpu.VMEM((8, count), F32),
            pltpu.VMEM((2 * local * count, cells), BF16),
            pltpu.VMEM((3, count + 2 * HALO, 2 * local * GROUP), BF16),
            pltpu.VMEM((2 * local * count, 6 * GROUP), BF16),
            pltpu.VMEM(state.shape, F32),
            pltpu.VMEM((2, local, HALO, GROUP), F32),
            pltpu.VMEM((2, local, HALO, GROUP), F32),
            pltpu.VMEM((xs, 2) + block, F32),
            pltpu.VMEM((ys, 2) + block, F32),
            pltpu.VMEM((ys, 2) + block, F32),
            pltpu.VMEM((xs, 2) + block, F32),
            pltpu.VMEM((2, ys) + block, F32),
            pltpu.VMEM((2, xs) + block, F32),
            sems((10,)), sems((2,)), sems((2,)),
            sems((xs, 2, CHUNKS)), sems((xs, 2, CHUNKS)),
            sems((ys, 2, CHUNKS)), sems((ys, 2, CHUNKS)),
            sems((ys, 2, CHUNKS)), sems((2, ys, CHUNKS)),
            sems((xs, 2, CHUNKS)), sems((2, xs, CHUNKS)),
        ],
        compiler_params=pltpu.CompilerParams(
            collective_id=0, has_side_effects=True, vmem_limit_bytes=60 * 2**20),
        cost_estimate=pl.CostEstimate(flops=3 * 10**9, bytes_accessed=4 * 2**20, transcendentals=0),
    )(lags, state, volume_kernel, minus, pick, place, neighbour.T, jscale.reshape(1, -1),
      send_left.reshape(1, -1), send_right.reshape(1, -1))
    residual = term - forcing
    return residual, state - pace.reshape(1, -1, 1) * residual


def solution(mesh):
    chips = mesh.shape["tm"] // 2
    xs = max(d for d in range(1, chips + 1) if chips % d == 0 and d * d <= chips)
    sizes = (xs, chips // xs, mesh.shape["space"])
    field = P("tm", "space", None)
    in_specs = (field, field, P("space"), P(), P("space", None), P("space"), P("space"))
    return jax.shard_map(functools.partial(local_step, sizes), mesh=mesh, in_specs=in_specs,
                         out_specs=(field, field), check_vma=False)
```

```python
import functools
import itertools

import jax
import jax.numpy as jnp
import numpy as np
from jax import lax
from jax.experimental import pallas as pl
from jax.experimental.pallas import tpu as pltpu
from jax.sharding import PartitionSpec as P

lift_factor = 2.0
step_factor = 0.2
CELLS = 256
HALO = 64
GROUP = 128
CHUNKS = 2
MESH = pl.DeviceIdType.MESH
F32, BF16 = jnp.float32, jnp.bfloat16


def face_nodes(face):
    end, axis = (3 if face % 2 else 0), face // 2
    cube = np.arange(64).reshape(4, 4, 4)
    return np.take(cube, end, axis=axis).reshape(-1)


def flux_table(source_rows, face):
    target = face_nodes(face)
    sign, axis = (1.0 if face % 2 else -1.0), face // 2
    mix = -np.eye(4)
    mix[1 + axis, 0] += sign
    mix[0, 1 + axis] += sign
    table = np.zeros((256, 4, 64))
    for a in range(16):
        for c in range(4):
            table[source_rows[c, a], :, target[a]] = 0.5 * lift_factor * mix[c]
    return table.reshape(256, 256)


def block_rows(face):
    return np.arange(4)[:, None] * 64 + face_nodes(face)[None, :]


def tables():
    pick = np.zeros((256, 384))
    for face in range(6):
        pick[block_rows(face).reshape(-1), face * 64 + np.arange(64)] = 1.0
    place = np.concatenate([
        flux_table(np.arange(64).reshape(4, 16) + 64 * (1 - f % 2), f)[:GROUP] for f in range(6)])
    minus = -sum(flux_table(block_rows(f), f) for f in range(6))
    return pick, place, minus


def lag_table(instances):
    lag = np.arange(-(instances - 1), instances)
    angle = np.pi * lag / instances
    sine = np.where(lag == 0, 1.0, np.sin(angle))
    value = 0.5 * (1.0 - 2.0 * (lag % 2)) * np.cos(angle) / sine
    return np.where(lag == 0, 0.0, value).astype(np.float32)


def halves(value):
    high = value.astype(BF16)
    return high, (value - high.astype(F32)).astype(BF16)


def dot(a, b):
    return jnp.dot(a, b, preferred_element_type=F32)


def kernel(sizes, lags_hbm, state, volume_hbm, minus_hbm, pick_hbm, place_hbm, neighbour_hbm, jscale_hbm,
           left_hbm, right_hbm, out, pace,
           lags, own, volume_kernel, minus, pick, place, neighbour, jscale, send_left, send_right,
           pack, split, traces, picked, acc, give, halo, g0, g1, p0, p1, r0, r1,
           load, hs, hr, s10, q10, s11, q11, s20, q20, s21, q21):
    xs, ys, zs = sizes
    local, count, _ = own.shape
    sub = g0.shape[4]
    chunks = g0.shape[2]
    quarter = count // 4
    parts = 2 * local
    instances = local * 2 * xs * ys
    t, z = lax.axis_index("tm"), lax.axis_index("space")
    core, chip = lax.rem(t, 2), lax.div(t, 2)
    x, y = lax.rem(chip, xs), lax.div(chip, xs)
    up, down = lax.rem(z + 1, zs), lax.rem(z + zs - 1, zs)

    def at(yy, xx, cc):
        return {"tm": (yy * xs + xx) * 2 + cc, "space": z}

    def turn(base, step, size):
        return lax.rem(base + step, size) if step else base

    def other(cc, step):
        return 1 - cc if step else cc

    row = [(dx, dc) for dx in range(xs) for dc in range(2)]
    column = [(dy, dc) for dy in range(ys) for dc in range(2)]
    peers = [at(y, turn(x, dx, xs), other(core, dc)) for dx, dc in row[1:]]
    peers += [at(turn(y, dy, ys), x, other(core, dc)) for dy, dc in column if dy]
    peers += [{"tm": t, "space": up}, {"tm": t, "space": down}]
    barrier = pltpu.get_barrier_semaphore()
    for peer in peers:
        pl.semaphore_signal(barrier, inc=1, device_id=peer, device_id_type=MESH)

    loads = [pltpu.make_async_copy(a, b, load.at[k]) for k, (a, b) in enumerate((
        (neighbour_hbm, neighbour), (jscale_hbm, jscale), (left_hbm, send_left), (right_hbm, send_right),
        (state, own), (pick_hbm, pick), (lags_hbm, lags), (volume_hbm, volume_kernel), (minus_hbm, minus),
        (place_hbm, place)))]
    loads[4].start()
    loads[4].wait()
    pl.semaphore_wait(barrier, len(peers))

    def rows(half, cc, k):
        return pl.ds(pl.multiple_of((2 * half + cc) * quarter + k * sub, sub), sub)

    plans = (
        (row, column, x, y, xs, ys, g0, p0, r0, s10, q10, s20, q20),
        (column, row, y, x, ys, xs, g1, p1, r1, s11, q11, s21, q21),
    )

    def target(half, first, second, cc):
        return at(second, first, cc) if half == 0 else at(first, second, cc)

    def first_copy(half, step, k, sending):
        (along, _, me, fixed, size, _, g, _, _, s, q, _, _), (d, dc) = plans[half], step
        mate, mate_core = turn(me, d, size), other(core, dc)
        slot = (me, core, k) if sending else (mate, mate_core, k)
        return pltpu.make_async_remote_copy(
            src_ref=own.at[:, rows(half, mate_core, k)], dst_ref=g.at[slot],
            send_sem=s.at[mate, mate_core, k], recv_sem=q.at[slot],
            device_id=target(half, mate, fixed, mate_core), device_id_type=MESH)

    def second_copy(half, step, k, sending):
        (_, _, fixed, me, _, size, _, p, r, _, _, s, q), (d, dc) = plans[half], step
        mate, mate_core = turn(me, d, size), other(core, dc)
        slot = (core, me, k) if sending else (mate_core, mate, k)
        return pltpu.make_async_remote_copy(
            src_ref=p.at[mate, mate_core, k], dst_ref=r.at[slot],
            send_sem=s.at[mate, mate_core, k], recv_sem=q.at[slot],
            device_id=target(half, fixed, mate, mate_core), device_id_type=MESH)

    firsts = []
    for k in range(chunks):
        far = [[(half, step, k) for step in plans[half][0] if step[0]] for half in (0, 1)]
        firsts += [one for pair in itertools.zip_longest(*far) for one in pair if one]
        firsts += [(half, (0, 1), k) for half in (0, 1)]
    for one in firsts:
        first_copy(*one, True).start()
    for one in loads[:4] + loads[5:]:
        one.start()

    for one in loads[:4]:
        one.wait()
    pack[0:6, :] = neighbour[...].astype(F32)
    pack[6:7, :] = jscale[...]
    pace[...] = step_factor / jscale[...]
    pack[7:8, 0:HALO] = send_left[...].astype(F32)
    pack[7:8, HALO:2 * HALO] = send_right[...].astype(F32)
    pack[7:8, 2 * HALO:] = jnp.zeros((1, count - 2 * HALO), F32)
    columns = jnp.transpose(pack[...])
    numbers = columns.astype(jnp.int32)
    scale = columns[:, 6:7]

    def hot(column, first, size, width):
        lanes = lax.broadcasted_iota(jnp.int32, (size, width), 1) + first
        return (column == lanes).astype(F32).astype(BF16)

    for i in range(local):
        high, low = halves(own[i])
        split[2 * i * count:(2 * i + 1) * count, :] = high
        split[(2 * i + 1) * count:(2 * i + 2) * count, :] = low
    loads[5].wait()
    for part in range(parts):
        found = dot(split[part * count:(part + 1) * count, :], pick[...]).astype(BF16)
        for axis in range(3):
            traces[axis, 0:count, part * GROUP:(part + 1) * GROUP] = found[:, axis * GROUP:(axis + 1) * GROUP]

    sent = dot(hot(numbers[0:2 * HALO, 7:8], 0, 2 * HALO, count), traces[1, 0:count, :])
    for i in range(local):
        value = sent[:, 2 * i * GROUP:(2 * i + 1) * GROUP] + sent[:, (2 * i + 1) * GROUP:(2 * i + 2) * GROUP]
        give[0, i] = value[0:HALO]
        give[1, i] = value[HALO:]

    def halo_copy(side):
        return pltpu.make_async_remote_copy(
            src_ref=give.at[side], dst_ref=halo.at[1 - side], send_sem=hs.at[side], recv_sem=hr.at[1 - side],
            device_id={"tm": t, "space": up if side else down}, device_id_type=MESH)

    for side in (0, 1):
        halo_copy(side).start()

    def gather(faces, width):
        for slot, face in enumerate(faces):
            found = dot(hot(numbers[:, face:face + 1], 0, count, width), traces[face // 2, 0:width, :]).astype(BF16)
            for part in range(parts):
                picked[part * count:(part + 1) * count, face * GROUP:(face + 1) * GROUP] = (
                    found[:, part * GROUP:(part + 1) * GROUP])

    def put(first, last, fresh=False):
        used = slice(first * GROUP, last * GROUP)
        for i in range(local):
            total = None if fresh else acc[i]
            for part in (2 * i, 2 * i + 1):
                term = dot(picked[part * count:(part + 1) * count, used], place[used, :])
                total = term if total is None else total + term
            acc[i] = total

    def volume():
        loads[7].wait()
        loads[8].wait()
        vh, vl = halves(volume_kernel[...] + minus[...].astype(F32))
        for i in range(local):
            high = split[2 * i * count:(2 * i + 1) * count, :]
            low = split[(2 * i + 1) * count:(2 * i + 2) * count, :]
            acc[i] = dot(high, vh) + dot(low, vh) + dot(high, vl)

    def partial(half, k):
        along, across, me, fixed, size, other_size, g, p, r, _, _, _, _ = plans[half]
        for step in along[1:]:
            first_copy(half, step, k, False).wait_recv()
        start = (2 * half + core) * quarter + k * sub

        def number(first, second, cc):
            return (((second * xs + first) if half == 0 else (first * xs + second)) * 2 + cc) * local

        origins = [(turn(me, d, size), other(core, dc)) for d, dc in along]
        for d, dc in [step for step in across if step[0]] + [(0, 1), (0, 0)]:
            mate, mate_core = turn(fixed, d, other_size), other(core, dc)
            base = number(me, mate, mate_core)
            weights = [[[lags[base + n - number(first, fixed, cc) - m + instances - 1] for m in range(local)]
                        for first, cc in origins] for n in range(local)]

            def step16(j, carry, d=d, dc=dc, mate=mate, mate_core=mate_core, weights=weights):
                here = pl.ds(pl.multiple_of(j * 16, 16), 16)
                totals = [None] * local
                for o, (first, cc) in enumerate(origins):
                    for m in range(local):
                        if o == 0:
                            value = own[m, pl.ds(pl.multiple_of(start + j * 16, 16), 16), :]
                        else:
                            value = g[first, cc, k, m, here, :]
                        for n in range(local):
                            term = weights[n][o][m] * value
                            totals[n] = term if totals[n] is None else totals[n] + term
                for n in range(local):
                    if d == 0 and dc == 0:
                        r[core, fixed, k, n, here, :] = totals[n]
                    else:
                        p[mate, mate_core, k, n, here, :] = totals[n]
                return carry

            lax.fori_loop(0, sub // 16, step16, 0)
            if (d, dc) != (0, 0):
                second_copy(half, (d, dc), k, True).start()

    volume()
    gather((0, 1), count)
    loads[6].wait()
    for k in range(chunks):
        for half in (0, 1):
            partial(half, k)
        if k == 0:
            gather((4, 5), count)
    loads[9].wait()
    put(0, 2)
    put(4, 6)

    for side in (0, 1):
        halo_copy(1 - side).wait_recv()
        first = count + side * HALO
        for i in range(local):
            high, low = halves(halo[side, i])
            traces[1, first:first + HALO, 2 * i * GROUP:(2 * i + 1) * GROUP] = high
            traces[1, first:first + HALO, (2 * i + 1) * GROUP:(2 * i + 2) * GROUP] = low
    gather((2, 3), count + 2 * HALO)
    put(2, 4)

    for k in range(chunks):
        for half in (0, 1):
            across, other_size, r = plans[half][1], plans[half][5], plans[half][8]
            for step in [s for s in across if s != (0, 0)]:
                second_copy(half, step, k, False).wait_recv()
            for cc in range(2):
                low = (2 * half + cc) * quarter + k * sub
                for i in range(local):
                    total = r[cc, 0, k, i]
                    for slot in range(1, other_size):
                        total = total + r[cc, slot, k, i]
                    out[i, low:low + sub, :] = total + scale[low:low + sub] * acc[i, low:low + sub, :]

    for one in firsts:
        first_copy(*one, True).wait_send()
    for side in (0, 1):
        halo_copy(side).wait_send()
    for k in range(chunks):
        for half in (0, 1):
            for step in [s for s in plans[half][1] if s != (0, 0)]:
                second_copy(half, step, k, True).wait_send()


def local_step(sizes, state, forcing, jscale, volume_kernel, neighbour, send_left, send_right):
    xs, ys, _ = sizes
    local, count, cells = state.shape
    quarter = count // 4
    sub = quarter // CHUNKS
    instances = local * 2 * xs * ys
    lags = jnp.asarray(lag_table(instances))
    pick, place, minus = [jnp.asarray(table.astype(np.float32), BF16) for table in tables()]
    block = (CHUNKS, local, sub, cells)
    sems = pltpu.SemaphoreType.DMA
    term, pace = pl.pallas_call(
        functools.partial(kernel, sizes),
        out_shape=(pltpu.VMEM(state.shape, F32), pltpu.VMEM((1, count), F32)),
        in_specs=[pl.BlockSpec(memory_space=pltpu.HBM)] * 10,
        out_specs=[pl.BlockSpec(memory_space=pltpu.VMEM)] * 2,
        scratch_shapes=[
            pltpu.SMEM(lags.shape, F32),
            pltpu.VMEM(state.shape, F32),
            pltpu.VMEM((cells, cells), F32),
            pltpu.VMEM(minus.shape, BF16),
            pltpu.VMEM(pick.shape, BF16),
            pltpu.VMEM(place.shape, BF16),
            pltpu.VMEM((6, count), jnp.int32),
            pltpu.VMEM((1, count), F32),
            pltpu.VMEM((1, HALO), jnp.int32),
            pltpu.VMEM((1, HALO), jnp.int32),
            pltpu.VMEM((8, count), F32),
            pltpu.VMEM((2 * local * count, cells), BF16),
            pltpu.VMEM((3, count + 2 * HALO, 2 * local * GROUP), BF16),
            pltpu.VMEM((2 * local * count, 6 * GROUP), BF16),
            pltpu.VMEM(state.shape, F32),
            pltpu.VMEM((2, local, HALO, GROUP), F32),
            pltpu.VMEM((2, local, HALO, GROUP), F32),
            pltpu.VMEM((xs, 2) + block, F32),
            pltpu.VMEM((ys, 2) + block, F32),
            pltpu.VMEM((ys, 2) + block, F32),
            pltpu.VMEM((xs, 2) + block, F32),
            pltpu.VMEM((2, ys) + block, F32),
            pltpu.VMEM((2, xs) + block, F32),
            sems((10,)), sems((2,)), sems((2,)),
            sems((xs, 2, CHUNKS)), sems((xs, 2, CHUNKS)),
            sems((ys, 2, CHUNKS)), sems((ys, 2, CHUNKS)),
            sems((ys, 2, CHUNKS)), sems((2, ys, CHUNKS)),
            sems((xs, 2, CHUNKS)), sems((2, xs, CHUNKS)),
        ],
        compiler_params=pltpu.CompilerParams(
            collective_id=0, has_side_effects=True, vmem_limit_bytes=60 * 2**20),
        cost_estimate=pl.CostEstimate(flops=3 * 10**9, bytes_accessed=4 * 2**20, transcendentals=0),
    )(lags, state, volume_kernel, minus, pick, place, neighbour.T, jscale.reshape(1, -1),
      send_left.reshape(1, -1), send_right.reshape(1, -1))
    residual = term - forcing
    return residual, state - pace.reshape(1, -1, 1) * residual


def solution(mesh):
    chips = mesh.shape["tm"] // 2
    xs = max(d for d in range(1, chips + 1) if chips % d == 0 and d * d <= chips)
    sizes = (xs, chips // xs, mesh.shape["space"])
    field = P("tm", "space", None)
    in_specs = (field, field, P("space"), P(), P("space", None), P("space"), P("space"))
    return jax.shard_map(functools.partial(local_step, sizes), mesh=mesh, in_specs=in_specs,
                         out_specs=(field, field), check_vma=False)
```
